256 devices in a mesh: gx: 32 (over z, x), gy: 8 (over y, core).
Axes of the slice: x: 4, y: 4, z: 8, core: 2. Of those that a mesh axis runs over, the one named last changes fastest.
Arguments:
- velocity: float32 [3, 8, 1536, 8192], P(None, None, 'gy', 'gx'), may hold values from -6 to 6
- metric_x: float32 [8192], P('gx'), may hold values from 0.3 to 3
- metric_y: float32 [1536], P('gy'), may hold values from 0.3 to 3
Outputs:
- derivs: float32 [3, 8, 1536, 8192], P(None, None, 'gy', 'gx')
- vorticity: float32 [8, 1536, 8192], P(None, 'gy', 'gx')
The draws below stay inside these ranges and needn't reach their ends.
All inputs are finite; a program needn't handle non-finite values.
Results may differ from the reference program's by a relative error of at most 0.00007.
Values sent between devices are 32-bit elements; how exact they have to be, the bound alone decides.
A program may use at most 64 MiB of HBM per device.

```python
import math
import jax
import jax.numpy as jnp
from jax import lax

DEPTH = 8
NX = 8192
NY = 1536


def level_of(key, shape, shards, smallest, largest):
    def one(dim, parts):
        heights = jax.random.uniform(jax.random.fold_in(jax.random.fold_in(key, 6), dim), (parts,), jnp.float32, smallest / len(shards), largest / len(shards))
        return jnp.repeat(jnp.exp(heights), shape[dim] // parts).reshape((-1,) + (1,) * (len(shape) - dim - 1))

    gain = one(*shards[0])
    for cut in shards[1:]:
        gain = gain * one(*cut)
    return gain


def normal_values(key, shape, width, bound, shards=(), held_as=jnp.bfloat16):
    array = width * jax.random.normal(key, shape, jnp.float32)
    if shards:
        array = array * level_of(key, shape, shards, -0.22, 0.18)
    return jnp.clip(array, -bound, bound).astype(held_as)


def setup_inputs(seed: int = 0) -> dict:
    streams_of = jax.random.split(jax.random.key(seed), 4)
    velocity = normal_values(streams_of[0], (3, DEPTH, NY, NX), 1.0, 6.0, ((2, 8), (3, 32)), jnp.float32)
    metric_x = jnp.clip(jnp.exp(math.log(3.0) - 2.3025851 * jax.random.uniform(streams_of[1], (NX,), jnp.float32) ** level_of(streams_of[1], (NX,), ((0, 32),), -0.2, 0.2)), 0.3, 3.0)
    metric_y = jnp.clip(jnp.exp(math.log(3.0) - 2.3025851 * jax.random.uniform(streams_of[2], (NY,), jnp.float32) ** level_of(streams_of[2], (NY,), ((0, 8),), -0.2, 0.2)), 0.3, 3.0)
    return {"velocity": velocity, "metric_x": metric_x, "metric_y": metric_y}


coupling = 1.0 / 3.0
near_weight = 7.0 / 9.0
far_weight = 1.0 / 36.0

def periodic_solve(right_side):
    lines = jnp.transpose(right_side)
    points = lines.shape[0]
    index = jnp.arange(points)
    kind = lines.dtype
    lower_diag = jnp.where(index > 0, coupling, 0.0).astype(kind)
    upper_diag = jnp.where(index < points - 1, coupling, 0.0).astype(kind)
    main_diag = jnp.where(index == 0, 2.0, jnp.where(index == points - 1, 1.0 + coupling * coupling, 1.0)).astype(kind)
    column = jnp.where(index == 0, -1.0, jnp.where(index == points - 1, coupling, 0.0)).astype(kind)
    both = jnp.concatenate([lines, column[:, None]], axis=1)
    solved = lax.linalg.tridiagonal_solve(lower_diag, main_diag, upper_diag, both)
    first = solved[:, :-1]
    helper = solved[:, -1]
    top = first[0] - coupling * first[points - 1]
    bottom = 1.0 + helper[0] - coupling * helper[points - 1]
    result = first - (top / bottom)[None, :] * helper[:, None]
    return jnp.transpose(result)

def line_slope(field):
    right_side = near_weight * (jnp.roll(field, -1, 1) - jnp.roll(field, 1, 1)) + far_weight * (jnp.roll(field, -2, 1) - jnp.roll(field, 2, 1))
    return periodic_solve(right_side)

def reference(velocity, metric_x, metric_y):
    planes = velocity.reshape((3 * DEPTH, NY, NX))
    slope = lax.map(line_slope, planes).reshape((3, DEPTH, NY, NX))
    derivs = slope * metric_x[None, None, None, :]
    upart = velocity[0]
    shear = (45.0 * (jnp.roll(upart, -1, 1) - jnp.roll(upart, 1, 1)) - 9.0 * (jnp.roll(upart, -2, 1) - jnp.roll(upart, 2, 1)) + (jnp.roll(upart, -3, 1) - jnp.roll(upart, 3, 1))) / 60.0
    vorticity = derivs[1] - metric_y[None, :, None] * shear
    return (derivs, vorticity)
```

```python
import numpy as np
import jax
import jax.numpy as jnp
from jax import lax
from jax.experimental import pallas as pl
from jax.experimental.pallas import tpu as pltpu
from jax.sharding import PartitionSpec as P

ratio = (np.sqrt(5.0) - 3.0) / 2.0
green = 1.0 / (1.0 + 2.0 * ratio / 3.0)
tail = green * 25.0 / 36.0
centre = green * (7.0 / 9.0 + ratio / 18.0)
MESH = pl.DeviceIdType.MESH
f32 = jnp.float32
bf16 = jnp.bfloat16


def powers_of_ratio(exponent, bits):
    value = jnp.ones(exponent.shape, f32)
    for bit in range(bits):
        factor = float(ratio ** (2**bit))
        factor = factor if abs(factor) > 1e-37 else 0.0
        value = value * jnp.where((exponent >> bit) & 1 == 1, factor, 1.0)
    return value


def band_matrix(points):
    source = lax.broadcasted_iota(jnp.int32, (points, points), 0)
    target = lax.broadcasted_iota(jnp.int32, (points, points), 1)
    distance = jnp.abs(target - source - 1)
    values = jnp.where(distance == 0, centre, tail * powers_of_ratio(distance, 9))
    values = jnp.where(source < points - 2, values, 0.0)
    high = values.astype(bf16)
    return high, (values - high.astype(f32)).astype(bf16)


def ring(axis):
    count = lax.axis_size(axis)
    me = lax.axis_index(axis)
    return lax.rem(me + 1, count), lax.rem(me + count - 1, count)


def local_kernel(
    velocity, metric_y, local, sheared, lefts, rights,
    my_line, band, u_rows, others, own, sent, from_left, from_right,
    my_sem, in_sem, y_send, y_recv, x_send, x_recv,
):
    fields, depth, rows, points = velocity.shape
    half = points // 2
    groups = rows // 64
    right, left = ring("gx")
    above, below = ring("gy")

    barrier = pltpu.get_barrier_semaphore()
    for axis, place in (("gx", right), ("gx", left), ("gy", above), ("gy", below)):
        pl.semaphore_signal(barrier, inc=1, device_id={axis: place}, device_id_type=MESH)

    loads = []
    for field in range(fields):
        if field == 0:
            target = u_rows.at[:, 8 : rows + 8]
        else:
            target = others.at[field - 1]
        load = pltpu.make_async_copy(velocity.at[field], target, in_sem.at[field])
        load.start()
        loads.append(load)

    my_load = pltpu.make_async_copy(metric_y, my_line, my_sem)
    my_load.start()
    band[0], band[1] = band_matrix(points)

    pl.semaphore_wait(barrier, 4)
    y_copies = [
        pltpu.make_async_remote_copy(
            velocity.at[0, :, rows - 8 : rows], u_rows.at[:, 0:8],
            y_send.at[0], y_recv.at[0], device_id={"gy": above}, device_id_type=MESH,
        ),
        pltpu.make_async_remote_copy(
            velocity.at[0, :, 0:8], u_rows.at[:, rows + 8 : rows + 16],
            y_send.at[1], y_recv.at[1], device_id={"gy": below}, device_id_type=MESH,
        ),
    ]
    for copy in y_copies:
        copy.start()

    lane = lax.broadcasted_iota(jnp.int32, (rows, half), 1)
    row = lax.broadcasted_iota(jnp.int32, (rows, half), 0)
    odd = lax.rem(lane, 2)
    slot = lane // 2 - lax.rem(row // 8, 8)
    small_odd = lax.broadcasted_iota(jnp.int32, (groups, 8, half), 2) % 2 == 1

    def lanes(x, shift):
        return pltpu.roll(x, shift % half, 2)

    x_copies = []
    for field in range(fields):
        loads[field].wait()

        def plane(z, packs):
            if field == 0:
                block = u_rows[z, 8 : rows + 8, :]
            else:
                block = others[field - 1, z]
            step = pltpu.roll(block, points - 2, 1) - block
            high = step.astype(bf16)
            low = (step - high.astype(f32)).astype(bf16)
            result = (
                jnp.dot(high, band[0], preferred_element_type=f32)
                + jnp.dot(low, band[0], preferred_element_type=f32)
                + jnp.dot(high, band[1], preferred_element_type=f32)
            )
            local[field, z] = result
            here = slot == z * 8

            def packed(values):
                return jnp.where(here, values, 0.0).reshape(groups, 8, 8, half).sum(axis=1)

            parts = (
                packed(jnp.take_along_axis(block[:, :half], 1 - odd, axis=1)),
                packed(jnp.take_along_axis(block[:, half:], half - 2 + odd, axis=1)),
                packed(jnp.broadcast_to(result[:, :1], (rows, half))),
                packed(jnp.broadcast_to(result[:, points - 1 :], (rows, half))),
            )
            return tuple(a + b for a, b in zip(packs, parts))

        zero = jnp.zeros((groups, 8, half), f32)
        first, last, start, end = lax.fori_loop(0, depth, plane, (zero,) * 4)
        own[0, field] = first
        own[1, field] = last
        sent[0, field] = jnp.where(
            small_odd, first, ratio * start + (tail * ratio) * (first - lanes(first, -1))
        )
        sent[1, field] = jnp.where(
            small_odd, last, ratio * end + (tail * ratio) * (lanes(last, -1) - last)
        )
        for side, place, target in ((0, left, from_right), (1, right, from_left)):
            copy = pltpu.make_async_remote_copy(
                sent.at[side, field], target.at[field],
                x_send.at[side, field], x_recv.at[side, field],
                device_id={"gx": place}, device_id_type=MESH,
            )
            copy.start()
            x_copies.append(copy)

    for copy in y_copies:
        copy.wait()
    square = (
        lax.broadcasted_iota(jnp.int32, (rows, rows), 0)
        == lax.broadcasted_iota(jnp.int32, (rows, rows), 1)
    )
    my_load.wait()
    my_row = my_line[...].reshape(1, rows)
    my_column = jnp.sum(jnp.where(square, my_row, 0.0), axis=1, keepdims=True)
    my_full = jnp.broadcast_to(my_column / 60.0, (rows, points))

    def shear_plane(z, carry):
        def shifted(k):
            return u_rows[z, 8 + k : rows + 8 + k, :]

        sheared[z] = my_full * (
            45.0 * (shifted(1) - shifted(-1))
            - 9.0 * (shifted(2) - shifted(-2))
            + (shifted(3) - shifted(-3))
        )
        return carry

    lax.fori_loop(0, depth, shear_plane, 0)

    for copy in x_copies:
        copy.wait()
    for field in range(fields):
        near = own[0, field]
        far = from_left[field]
        far_edge = lanes(far, -1)
        straddle = near - far_edge
        total = far + tail * straddle + (tail * ratio) * (lanes(near, -1) - far_edge)
        lefts[field] = jnp.where(
            small_odd, lanes(total + (centre - tail) * straddle, 1), total
        )
        near = own[1, field]
        far = from_right[field]
        far_edge = lanes(far, -1)
        straddle = far_edge - near
        total = far + tail * straddle + (tail * ratio) * (far_edge - lanes(near, -1))
        rights[field] = jnp.where(
            small_odd, lanes(total + (centre - tail) * straddle, 1), total
        )


def finish_kernel(local, sheared, lefts, rights, metric_x, derivs, vorticity, staged, out_sem):
    fields, depth, rows, points = derivs.shape
    half = points // 2
    groups = rows // 64
    lane = lax.broadcasted_iota(jnp.int32, (rows, half), 1)
    row = lax.broadcasted_iota(jnp.int32, (rows, half), 0)
    slot = 2 * lax.rem(row // 8, 8)
    left_slot = slot + jnp.where(lane == 0, 1, 0)
    right_slot = slot + jnp.where(lane == half - 1, 1, 0)
    mx = metric_x[...].reshape(1, points)
    column = lax.broadcasted_iota(jnp.int32, (1, half), 1)
    left_powers = powers_of_ratio(column, 7)
    right_powers = powers_of_ratio(half - 1 - column, 7)

    def spread(pack, index):
        wide = jnp.broadcast_to(pack[:, None], (groups, 8, 8, half)).reshape(rows, half)
        return jnp.take_along_axis(wide, index, axis=1)

    def copies(z):
        out = [
            pltpu.make_async_copy(staged.at[field, z], derivs.at[field, z], out_sem.at[field, z])
            for field in range(fields)
        ]
        out.append(pltpu.make_async_copy(staged.at[fields, z], vorticity.at[z], out_sem.at[fields, z]))
        return out

    def plane(z, carry):
        sends = copies(z)
        for field in range(fields):
            block = local[field, z]
            low = block[:, :half] + spread(lefts[field], left_slot + 16 * z) * left_powers
            high = block[:, half:] + spread(rights[field], right_slot + 16 * z) * right_powers
            low = low * mx[:, :half]
            high = high * mx[:, half:]
            staged[field, z, :, :half] = low
            staged[field, z, :, half:] = high
            sends[field].start()
            if field == 1:
                staged[fields, z, :, :half] = low - sheared[z, :, :half]
                staged[fields, z, :, half:] = high - sheared[z, :, half:]
                sends[fields].start()
        return carry

    lax.fori_loop(0, depth, plane, 0)

    def drain(z, carry):
        for copy in copies(z):
            copy.wait()
        return carry

    lax.fori_loop(0, depth, drain, 0)


def per_device(velocity, metric_x, metric_y):
    fields, depth, rows, points = velocity.shape
    half = points // 2
    groups = rows // 64
    packs = (fields, groups, 8, half)
    anywhere = pl.BlockSpec(memory_space=pl.ANY)
    hbm = pl.BlockSpec(memory_space=pltpu.HBM)
    vmem = pl.BlockSpec(memory_space=pltpu.VMEM)
    local, sheared, lefts, rights = pl.pallas_call(
        local_kernel,
        out_shape=(
            OUT((fields, depth, rows, points), f32),
            OUT((depth, rows, points), f32),
            OUT(packs, f32),
            OUT(packs, f32),
        ),
        in_specs=[hbm, hbm],
        out_specs=(vmem,) * 4,
        scratch_shapes=[
            pltpu.VMEM((rows,), f32),
            pltpu.VMEM((2, points, points), bf16),
            pltpu.VMEM((depth, rows + 16, points), f32),
            pltpu.VMEM((fields - 1, depth, rows, points), f32),
            pltpu.VMEM((2,) + packs, f32),
            pltpu.VMEM((2,) + packs, f32),
            pltpu.VMEM(packs, f32),
            pltpu.VMEM(packs, f32),
            pltpu.SemaphoreType.DMA(()),
            pltpu.SemaphoreType.DMA((fields,)),
            pltpu.SemaphoreType.DMA((2,)),
            pltpu.SemaphoreType.DMA((2,)),
            pltpu.SemaphoreType.DMA((2, fields)),
            pltpu.SemaphoreType.DMA((2, fields)),
        ],
        compiler_params=pltpu.CompilerParams(
            collective_id=0, has_side_effects=True, vmem_limit_bytes=24 * 1024 * 1024
        ),
        name="local",
    )(
        pltpu.with_memory_space_constraint(velocity, pltpu.HBM),
        pltpu.with_memory_space_constraint(metric_y, pltpu.HBM),
    )
    return pl.pallas_call(
        finish_kernel,
        out_shape=(
            jax.ShapeDtypeStruct((fields, depth, rows, points), f32),
            jax.ShapeDtypeStruct((depth, rows, points), f32),
        ),
        in_specs=[vmem] * 5,
        out_specs=(anywhere, anywhere),
        scratch_shapes=[
            pltpu.VMEM((fields + 1, depth, rows, points), f32),
            pltpu.SemaphoreType.DMA((fields + 1, depth)),
        ],
        compiler_params=pltpu.CompilerParams(vmem_limit_bytes=24 * 1024 * 1024),
        name="finish",
    )(local, sheared, lefts, rights, metric_x)


OUT = pltpu.VMEM


def solution(mesh):
    in_specs = (P(None, None, "gy", "gx"), P("gx"), P("gy"))
    out_specs = (P(None, None, "gy", "gx"), P(None, "gy", "gx"))
    return jax.shard_map(
        per_device, mesh=mesh, in_specs=in_specs, out_specs=out_specs, check_vma=False
    )
```

```python
import numpy as np
import jax
import jax.numpy as jnp
from jax import lax
from jax.experimental import pallas as pl
from jax.experimental.pallas import tpu as pltpu
from jax.sharding import PartitionSpec as P

ratio = (np.sqrt(5.0) - 3.0) / 2.0
green = 1.0 / (1.0 + 2.0 * ratio / 3.0)
tail = green * 25.0 / 36.0
centre = green * (7.0 / 9.0 + ratio / 18.0)
MESH = pl.DeviceIdType.MESH
f32 = jnp.float32
bf16 = jnp.bfloat16
PAD = 8
LOAD_PARTS = 2
BATCH = 8
EDGE_ROWS = 64
BLOCK = 16
PER_TILE = 6
STRETCH = 1.8203296661376953


def powers_of_ratio(exponent, bits):
    value = jnp.ones(exponent.shape, f32)
    for bit in range(bits):
        factor = float(ratio ** (2**bit))
        factor = factor if abs(factor) > 1e-37 else 0.0
        value = value * jnp.where((exponent >> bit) & 1 == 1, factor, 1.0)
    return value


def halves(values):
    high = values.astype(bf16)
    return high, (values - high.astype(f32)).astype(bf16)


def band_matrix(points):
    source = lax.broadcasted_iota(jnp.int32, (points, points), 0)
    target = lax.broadcasted_iota(jnp.int32, (points, points), 1)
    distance = jnp.abs(target - source - 1)
    values = jnp.where(distance == 0, centre, tail * powers_of_ratio(distance, 7))
    return jnp.where((source < points - 2) & (distance < 128), values, 0.0)


def correction_matrix(points):
    half = points // 2
    source = lax.broadcasted_iota(jnp.int32, (points, points), 0)
    target = lax.broadcasted_iota(jnp.int32, (points, points), 1)
    distance = jnp.where(source < half, target, points - 1 - target)
    edge = jnp.where(distance == 0, 1.0, 0.0)
    decay = jnp.where(distance < 128, STRETCH * powers_of_ratio(distance, 7), 0.0)
    return jnp.where(source % 2 == 1, edge, decay), source


def ring(axis):
    count = lax.axis_size(axis)
    me = lax.axis_index(axis)
    return lax.rem(me + 1, count), lax.rem(me + count - 1, count)


def local_kernel(
    velocity, metric_y, local, sheared, strips, spreads,
    my_line, band, held, sent, own, arrived,
    my_sem, in_sem, y_send, y_recv, x_send, x_recv,
):
    fields, depth, rows, points = velocity.shape
    half = points // 2
    right, left = ring("gx")
    above, below = ring("gy")
    planes = depth // LOAD_PARTS

    barrier = pltpu.get_barrier_semaphore()
    for axis, place in (("gx", right), ("gx", left), ("gy", above), ("gy", below)):
        pl.semaphore_signal(barrier, inc=1, device_id={axis: place}, device_id_type=MESH)

    def load(part):
        field = part // LOAD_PARTS
        span = pl.ds((part % LOAD_PARTS) * planes, planes)
        return [
            pltpu.make_async_copy(
                velocity.at[field, span, :, side * half : (side + 1) * half],
                held.at[field, side, span, PAD : PAD + rows],
                in_sem.at[part, side],
            )
            for side in range(2)
        ]

    for part in range(fields * LOAD_PARTS):
        for copy in load(part):
            copy.start()
    my_load = pltpu.make_async_copy(metric_y, my_line, my_sem)
    my_load.start()

    high, low = halves(band_matrix(points))
    band[0:points] = high
    band[points : 2 * points] = high
    band[2 * points :] = low
    decay, source = correction_matrix(points)
    for z in range(depth):
        spreads[z] = jnp.where(source // 2 % depth == z, decay, 0.0).astype(bf16)

    lane = lax.broadcasted_iota(jnp.int32, (8, half), 1)
    odd = lane % 2 == 1
    scale = tail * (1.0 + ratio)
    spread = scale * (1.0 - ratio)
    left_weight = jnp.where(lane == 0, -scale * ratio, spread * powers_of_ratio(lane, 7))
    right_weight = jnp.where(
        lane == half - 1, scale * ratio, -spread * powers_of_ratio(half - 1 - lane, 7)
    )

    wide_odd = lax.broadcasted_iota(jnp.int32, (EDGE_ROWS // 8, 8, half), 2) % 2
    edge_lanes = (1 - wide_odd, half - 2 + wide_odd)

    def edges(part, carry):
        for copy in load(part):
            copy.wait()
        field = part // LOAD_PARTS

        def plane(step, carry):
            z = (part % LOAD_PARTS) * planes + step
            masks = [lane // 2 == within * 8 + z for within in range(PER_TILE)]
            for start in range(0, rows, EDGE_ROWS):
                for side, weight in ((0, left_weight), (1, right_weight)):
                    block = held[field, side, z, PAD + start : PAD + start + EDGE_ROWS, :]
                    block = block.reshape(EDGE_ROWS // 8, 8, half)
                    edge = jnp.take_along_axis(block, edge_lanes[side], axis=2)
                    total = jnp.sum(block * weight, axis=2, keepdims=True)
                    value = jnp.where(odd, edge, total)
                    for index in range(EDGE_ROWS // 8):
                        group = start // 8 + index
                        tile, within = divmod(group // 2, PER_TILE)
                        place = (side, field, tile, pl.ds((group % 2) * 8, 8))
                        pltpu.store(sent.at[place], value[index], mask=masks[within])
                        pltpu.store(own.at[place], edge[index], mask=masks[within])
            return carry

        return lax.fori_loop(0, planes, plane, carry)

    lax.fori_loop(0, fields * LOAD_PARTS, edges, 0)

    pl.semaphore_wait(barrier, 4)
    x_copies = [
        pltpu.make_async_remote_copy(
            sent.at[side], arrived.at[1 - side], x_send.at[side], x_recv.at[1 - side],
            device_id={"gx": place}, device_id_type=MESH,
        )
        for side, place in ((0, left), (1, right))
    ]
    y_copies = [
        pltpu.make_async_remote_copy(
            velocity.at[0, :, first : first + PAD, side * half : (side + 1) * half],
            held.at[0, side, :, target : target + PAD],
            y_send.at[way, side], y_recv.at[way, side],
            device_id={"gy": place}, device_id_type=MESH,
        )
        for way, (first, target, place) in enumerate(
            ((rows - PAD, 0, above), (0, rows + PAD, below))
        )
        for side in range(2)
    ]
    for copy in x_copies + y_copies:
        copy.start()

    many = BATCH * rows
    def product(index, carry):
        field = index // (depth // BATCH)
        z = (index % (depth // BATCH)) * BATCH
        first = held[field, 0, pl.ds(z, BATCH), PAD : PAD + rows, :].reshape(many, half)
        second = held[field, 1, pl.ds(z, BATCH), PAD : PAD + rows, :].reshape(many, half)
        step = pltpu.roll(jnp.concatenate([first, second], axis=1), points - 2, 1)
        step = step - jnp.concatenate([first, second], axis=1)
        high, low = halves(step)
        result = jnp.dot(
            jnp.concatenate([high, low, high], axis=1), band[...], preferred_element_type=f32
        )
        local[field, pl.ds(z, BATCH)] = result.reshape(BATCH, rows, points)
        return carry

    lax.fori_loop(0, fields * depth // BATCH, product, 0)

    my_load.wait()
    square = (
        lax.broadcasted_iota(jnp.int32, (rows, rows), 0)
        == lax.broadcasted_iota(jnp.int32, (rows, rows), 1)
    )
    my_row = my_line[...].reshape(1, rows)
    my_column = jnp.sum(jnp.where(square, my_row, 0.0), axis=1, keepdims=True) / 60.0

    for copy in y_copies:
        copy.wait()

    def shear_plane(z, carry):
        for side in range(2):

            def shifted(k):
                return held[0, side, z, PAD + k : rows + PAD + k, :]

            sheared[z, :, side * half : (side + 1) * half] = my_column * (
                45.0 * (shifted(1) - shifted(-1))
                - 9.0 * (shifted(2) - shifted(-2))
                + (shifted(3) - shifted(-3))
            )
        return carry

    lax.fori_loop(0, depth, shear_plane, 0)

    for copy in x_copies:
        copy.wait()
    shape = arrived.shape[1:]
    small_odd = small_lanes(shape) % 2 == 1
    strip_lanes = small_lanes((BLOCK, half)) // BLOCK
    for side in range(2):
        sign = 1.0 if side == 0 else -1.0
        far, near = arrived[side], own[side]
        far_edge = pltpu.roll(far, half - 1, 3)
        straddle = sign * (near - far_edge)
        jump = sign * (pltpu.roll(near, half - 1, 3) - far_edge)
        value = jnp.where(
            small_odd,
            pltpu.roll((centre - tail) * straddle, 1, 3),
            (far + tail * straddle + (tail * ratio) * jump) * (1.0 / STRETCH),
        )
        for field in range(fields):
            for block in range(rows // BLOCK):
                tile, within = divmod(block, PER_TILE)
                start = field * rows + block * BLOCK
                piece = jnp.where(strip_lanes == within, value[field, tile], 0.0)
                high, low = halves(piece)
                strips[start : start + BLOCK, side * half : (side + 1) * half] = high
                strips[start : start + BLOCK, points + side * half : points + (side + 1) * half] = low


def small_lanes(shape):
    return lax.broadcasted_iota(jnp.int32, shape, len(shape) - 1)


def finish_kernel(
    local, sheared, strips, spreads, metric_x, derivs, vorticity, staged, out_sem
):
    fields, depth, rows, points = derivs.shape
    mx = metric_x[...].reshape(1, points)

    def copies(z):
        out = [
            pltpu.make_async_copy(staged.at[field, z], derivs.at[field, z], out_sem.at[field, z])
            for field in range(fields)
        ]
        out.append(pltpu.make_async_copy(staged.at[fields, z], vorticity.at[z], out_sem.at[fields, z]))
        return out

    def plane(z, carry):
        sends = copies(z)
        change = jnp.dot(
            strips[:, :points], spreads[z], preferred_element_type=f32
        ) + jnp.dot(strips[:, points:], spreads[z], preferred_element_type=f32)
        for field in range(fields):
            value = (local[field, z] + change[field * rows : (field + 1) * rows]) * mx
            staged[field, z] = value
            if field == 1:
                staged[fields, z] = value - sheared[z]
        for copy in sends:
            copy.start()
        return carry

    lax.fori_loop(0, depth, plane, 0)

    def drain(z, carry):
        for copy in copies(z):
            copy.wait()
        return carry

    lax.fori_loop(0, depth, drain, 0)


def per_device(velocity, metric_x, metric_y):
    fields, depth, rows, points = velocity.shape
    half = points // 2
    packs = (fields, 2, BLOCK, half)
    parts = fields * LOAD_PARTS
    anywhere = pl.BlockSpec(memory_space=pl.ANY)
    hbm = pl.BlockSpec(memory_space=pltpu.HBM)
    vmem = pl.BlockSpec(memory_space=pltpu.VMEM)
    local, sheared, strips, spreads = pl.pallas_call(
        local_kernel,
        out_shape=(
            pltpu.VMEM((fields, depth, rows, points), f32),
            pltpu.VMEM((depth, rows, points), f32),
            pltpu.VMEM((fields * rows, 2 * points), bf16),
            pltpu.VMEM((depth, points, points), bf16),
        ),
        in_specs=[hbm, hbm],
        out_specs=(vmem,) * 4,
        scratch_shapes=[
            pltpu.VMEM((rows,), f32),
            pltpu.VMEM((3 * points, points), bf16),
            pltpu.VMEM((fields, 2, depth, rows + 2 * PAD, half), f32),
            pltpu.VMEM((2,) + packs, f32),
            pltpu.VMEM((2,) + packs, f32),
            pltpu.VMEM((2,) + packs, f32),
            pltpu.SemaphoreType.DMA(()),
            pltpu.SemaphoreType.DMA((parts, 2)),
            pltpu.SemaphoreType.DMA((2, 2)),
            pltpu.SemaphoreType.DMA((2, 2)),
            pltpu.SemaphoreType.DMA((2,)),
            pltpu.SemaphoreType.DMA((2,)),
        ],
        compiler_params=pltpu.CompilerParams(
            collective_id=0, has_side_effects=True, vmem_limit_bytes=24 * 1024 * 1024
        ),
        name="local",
    )(
        pltpu.with_memory_space_constraint(velocity, pltpu.HBM),
        pltpu.with_memory_space_constraint(metric_y, pltpu.HBM),
    )
    return pl.pallas_call(
        finish_kernel,
        out_shape=(
            jax.ShapeDtypeStruct((fields, depth, rows, points), f32),
            jax.ShapeDtypeStruct((depth, rows, points), f32),
        ),
        in_specs=[vmem] * 5,
        out_specs=(anywhere, anywhere),
        scratch_shapes=[
            pltpu.VMEM((fields + 1, depth, rows, points), f32),
            pltpu.SemaphoreType.DMA((fields + 1, depth)),
        ],
        compiler_params=pltpu.CompilerParams(vmem_limit_bytes=24 * 1024 * 1024),
        name="finish",
    )(local, sheared, strips, spreads, metric_x)


def solution(mesh):
    in_specs = (P(None, None, "gy", "gx"), P("gx"), P("gy"))
    out_specs = (P(None, None, "gy", "gx"), P(None, "gy", "gx"))
    return jax.shard_map(
        per_device, mesh=mesh, in_specs=in_specs, out_specs=out_specs, check_vma=False
    )
```

```python
import numpy as np
import jax
import jax.numpy as jnp
from jax import lax
from jax.experimental import pallas as pl
from jax.experimental.pallas import tpu as pltpu
from jax.sharding import PartitionSpec as P

ratio = (np.sqrt(5.0) - 3.0) / 2.0
green = 1.0 / (1.0 + 2.0 * ratio / 3.0)
tail = green * 25.0 / 36.0
centre = green * (7.0 / 9.0 + ratio / 18.0)
MESH = pl.DeviceIdType.MESH
f32 = jnp.float32
bf16 = jnp.bfloat16
PAD = 8
LOAD_PARTS = 2
BATCH = 8
EDGE_PLANES = 2
MEET = 1
FINISH_PLANES = 2
BLOCK = 16
PER_TILE = 6
STRETCH = 1.8203296661376953


def powers_of_ratio(exponent, bits):
    value = jnp.ones(exponent.shape, f32)
    for bit in range(bits):
        factor = float(ratio ** (2**bit))
        factor = factor if abs(factor) > 1e-37 else 0.0
        value = value * jnp.where((exponent >> bit) & 1 == 1, factor, 1.0)
    return value


def halves(values):
    high = values.astype(bf16)
    return high, (values - high.astype(f32)).astype(bf16)


def band_matrix(points):
    source = lax.broadcasted_iota(jnp.int32, (points, points), 0)
    target = lax.broadcasted_iota(jnp.int32, (points, points), 1)
    distance = jnp.abs(target - source - 1)
    values = jnp.where(distance == 0, centre, tail * powers_of_ratio(distance, 7))
    return jnp.where((source < points - 2) & (distance < 128), values, 0.0)


def correction_matrix(points):
    half = points // 2
    source = lax.broadcasted_iota(jnp.int32, (points, points), 0)
    target = lax.broadcasted_iota(jnp.int32, (points, points), 1)
    distance = jnp.where(source < half, target, points - 1 - target)
    edge = jnp.where(distance == 0, 1.0, 0.0)
    decay = jnp.where(distance < 128, STRETCH * powers_of_ratio(distance, 7), 0.0)
    second = source % 2 == jnp.where(source < half, 1, 0)
    return jnp.where(second, edge, decay), source


def ring(axis):
    count = lax.axis_size(axis)
    me = lax.axis_index(axis)
    return lax.rem(me + 1, count), lax.rem(me + count - 1, count)


def local_kernel(
    velocity, metric_y, local, sheared, strips, spreads,
    my_line, band, held, sent, own, arrived,
    ready, my_sem, in_sem, y_send, y_recv, x_send, x_recv,
):
    fields, depth, rows, points = velocity.shape
    half = points // 2
    right, left = ring("gx")
    above, below = ring("gy")
    seam = lax.axis_index("gx") == 0
    last = lax.axis_index("gx") == lax.axis_size("gx") - 1
    barrier = pltpu.get_barrier_semaphore()
    for axis, place in (("gy", above), ("gy", below), ("gx", left)):
        pl.semaphore_signal(barrier, inc=1, device_id={axis: place}, device_id_type=MESH)

    @pl.when(jnp.logical_not(last))
    def greet_right():
        pl.semaphore_signal(barrier, inc=1, device_id={"gx": right}, device_id_type=MESH)

    planes = depth // LOAD_PARTS

    def load(side, part):
        field = part // LOAD_PARTS
        span = pl.ds((part % LOAD_PARTS) * planes, planes)
        return pltpu.make_async_copy(
            velocity.at[field, span, :, side * half : (side + 1) * half],
            held.at[field, side, span, PAD : PAD + rows],
            in_sem.at[side, part],
        )

    parts = fields * LOAD_PARTS
    for part in range(parts):
        load(1, part).start()
    my_load = pltpu.make_async_copy(metric_y, my_line, my_sem)

    high, low = halves(band_matrix(points))
    band[0:points] = high
    band[points : 2 * points] = high
    band[2 * points :] = low

    lane = lax.broadcasted_iota(jnp.int32, (8, half), 1)
    odd = lane % 2 == 1
    scale = tail * (1.0 + ratio)
    spread = scale * (1.0 - ratio)
    left_weight = jnp.where(lane == 0, -scale * ratio, spread * powers_of_ratio(lane, 7))
    right_weight = jnp.where(
        lane == half - 1, scale * ratio, -spread * powers_of_ratio(half - 1 - lane, 7)
    )

    def edges(side, after):
        weight = right_weight if side else left_weight

        def piece(part, carry):
            load(side, part).wait()
            if side:

                @pl.when(part == parts - 2)
                def start_others():
                    for other in range(parts):
                        load(0, other).start()
                    my_load.start()

            field = part // LOAD_PARTS

            def pair(step, carry):
                first = (part % LOAD_PARTS) * planes + step * EDGE_PLANES
                for z in [first + k for k in range(EDGE_PLANES)]:
                    groups = range(rows // 8)
                    blocks = [held[field, side, z, PAD + g * 8 : PAD + g * 8 + 8, :] for g in groups]
                    totals = [jnp.sum(block * weight, axis=1, keepdims=True) for block in blocks]
                    masks = [lane // 2 == within * 8 + z for within in range(PER_TILE)]
                    for group, block, total in zip(groups, blocks, totals):
                        tile, within = divmod(group // 2, PER_TILE)
                        edge = pltpu.roll(block, within * BLOCK + 2 * z + 2 * side, 1)
                        value = jnp.where(odd, edge, total) if side else jnp.where(odd, total, edge)
                        place = (side, field, tile, pl.ds((group % 2) * 8, 8))
                        pltpu.store(sent.at[place], value, mask=masks[within])
                        pltpu.store(own.at[place], edge, mask=masks[within])
                return carry

            return lax.fori_loop(0, planes // EDGE_PLANES, pair, carry)

        def whole(field, carry):
            lax.fori_loop(field * LOAD_PARTS, (field + 1) * LOAD_PARTS, piece, 0)
            after(field)
            return carry

        lax.fori_loop(0, fields, whole, 0)

    def x_copy(side, field):
        return pltpu.make_async_remote_copy(
            sent.at[side, field], arrived.at[1 - side, field],
            x_send.at[side, field], x_recv.at[1 - side, field],
            device_id={"gx": right if side else left}, device_id_type=MESH,
        )

    y_copies = [
        pltpu.make_async_remote_copy(
            velocity.at[0, :, first : first + PAD, side * half : (side + 1) * half],
            held.at[0, side, :, target : target + PAD],
            y_send.at[way, side], y_recv.at[way, side],
            device_id={"gy": place}, device_id_type=MESH,
        )
        for way, (first, target, place) in enumerate(
            ((rows - PAD, 0, above), (0, rows + PAD, below))
        )
        for side in range(2)
    ]

    def send_right(field):
        @pl.when(field == MEET)
        def meet():
            @pl.when(seam)
            def meet_three():
                pl.semaphore_wait(barrier, 3)

            @pl.when(jnp.logical_not(seam))
            def meet_four():
                pl.semaphore_wait(barrier, 4)

            @pl.when(last)
            def invite():
                pl.semaphore_signal(ready, inc=1, device_id={"gx": right}, device_id_type=MESH)

            for earlier in range(MEET):
                x_copy(1, earlier).start()

        @pl.when(field >= MEET)
        def send():
            x_copy(1, field).start()

    def send_left(field):
        @pl.when(field == 0)
        def first():
            for copy in y_copies:
                copy.start()

        @pl.when(jnp.logical_not(seam))
        def send():
            x_copy(0, field).start()

    edges(1, send_right)
    edges(0, send_left)

    decay, source = correction_matrix(points)
    for z in range(depth):
        spreads[z] = jnp.where(source // 2 % depth == z, decay, 0.0).astype(bf16)

    many = BATCH * rows
    def product(index, carry):
        field = index // (depth // BATCH)
        z = (index % (depth // BATCH)) * BATCH
        first = held[field, 0, pl.ds(z, BATCH), PAD : PAD + rows, :].reshape(many, half)
        second = held[field, 1, pl.ds(z, BATCH), PAD : PAD + rows, :].reshape(many, half)
        step = pltpu.roll(jnp.concatenate([first, second], axis=1), points - 2, 1)
        step = step - jnp.concatenate([first, second], axis=1)
        high, low = halves(step)
        result = jnp.dot(
            jnp.concatenate([high, low, high], axis=1), band[...], preferred_element_type=f32
        )
        local[field, pl.ds(z, BATCH)] = result.reshape(BATCH, rows, points)
        return carry

    my_load.wait()
    square = (
        lax.broadcasted_iota(jnp.int32, (rows, rows), 0)
        == lax.broadcasted_iota(jnp.int32, (rows, rows), 1)
    )
    my_row = my_line[...].reshape(1, rows)
    my_column = jnp.sum(jnp.where(square, my_row, 0.0), axis=1, keepdims=True) / 60.0

    def shear_rows(z, start, stop):
        for side in range(2):

            def shifted(k):
                return held[0, side, z, PAD + start + k : PAD + stop + k, :]

            sheared[z, start:stop, side * half : (side + 1) * half] = my_column[start:stop] * (
                45.0 * (shifted(1) - shifted(-1))
                - 9.0 * (shifted(2) - shifted(-2))
                + (shifted(3) - shifted(-3))
            )

    def shear_inner(z, carry):
        shear_rows(z, PAD, rows - PAD)
        return carry

    lax.fori_loop(0, depth, shear_inner, 0)

    lax.fori_loop(0, fields * depth // BATCH, product, 0)

    @pl.when(seam)
    def send_late():
        pl.semaphore_wait(ready, 1)
        for field in range(fields):
            x_copy(0, field).start()

    for copy in y_copies:
        copy.wait()

    for z in range(depth):
        shear_rows(z, 0, PAD)
        shear_rows(z, rows - PAD, rows)

    shape = arrived.shape[1:]
    small_odd = small_lanes(shape) % 2 == 1
    strip_lanes = small_lanes((BLOCK, half)) // BLOCK
    for side in (1, 0):
        for field in range(fields):
            x_copy(1 - side, field).wait_recv()
        far, near = arrived[side], own[side]
        turn, sign = (half - 1, 1.0) if side == 0 else (1, -1.0)
        straddle = sign * (near - far)
        jump = sign * (near - pltpu.roll(far, turn, 3))
        value = jnp.where(
            small_odd == (side == 0),
            (centre - tail) * straddle,
            (far + tail * pltpu.roll(straddle, turn, 3) + (tail * ratio) * jump)
            * (1.0 / STRETCH),
        )
        for field in range(fields):
            for block in range(rows // BLOCK):
                tile, within = divmod(block, PER_TILE)
                start = field * rows + block * BLOCK
                piece = jnp.where(strip_lanes == within, value[field, tile], 0.0)
                high, low = halves(piece)
                strips[start : start + BLOCK, side * half : (side + 1) * half] = high
                strips[start : start + BLOCK, points + side * half : points + (side + 1) * half] = low
    for side in range(2):
        for field in range(fields):
            x_copy(side, field).wait_send()


def small_lanes(shape):
    return lax.broadcasted_iota(jnp.int32, shape, len(shape) - 1)


def finish_kernel(
    local, sheared, strips, spreads, metric_x, derivs, vorticity, staged, out_sem
):
    fields, depth, rows, points = derivs.shape
    mx = metric_x[...].reshape(1, points)

    def copies(z):
        out = [
            pltpu.make_async_copy(staged.at[field, z], derivs.at[field, z], out_sem.at[0])
            for field in range(fields)
        ]
        out.append(pltpu.make_async_copy(staged.at[fields, z], vorticity.at[z], out_sem.at[1]))
        return out

    def planes(step, carry):
        for z in [step * FINISH_PLANES + k for k in range(FINISH_PLANES)]:
            change = jnp.dot(
                strips[:, :points], spreads[z], preferred_element_type=f32
            ) + jnp.dot(strips[:, points:], spreads[z], preferred_element_type=f32)
            for field in range(fields):
                value = (local[field, z] + change[field * rows : (field + 1) * rows]) * mx
                staged[field, z] = value
                if field == 1:
                    staged[fields, z] = value - sheared[z]
            for copy in copies(z):
                copy.start()
        return carry

    lax.fori_loop(0, depth // FINISH_PLANES, planes, 0)

    pltpu.make_async_copy(staged.at[0:fields], derivs, out_sem.at[0]).wait()
    pltpu.make_async_copy(staged.at[fields], vorticity, out_sem.at[1]).wait()


def per_device(velocity, metric_x, metric_y):
    fields, depth, rows, points = velocity.shape
    half = points // 2
    packs = (fields, 2, BLOCK, half)
    parts = fields * LOAD_PARTS
    anywhere = pl.BlockSpec(memory_space=pl.ANY)
    hbm = pl.BlockSpec(memory_space=pltpu.HBM)
    vmem = pl.BlockSpec(memory_space=pltpu.VMEM)
    local, sheared, strips, spreads = pl.pallas_call(
        local_kernel,
        out_shape=(
            pltpu.VMEM((fields, depth, rows, points), f32),
            pltpu.VMEM((depth, rows, points), f32),
            pltpu.VMEM((fields * rows, 2 * points), bf16),
            pltpu.VMEM((depth, points, points), bf16),
        ),
        in_specs=[hbm, hbm],
        out_specs=(vmem,) * 4,
        scratch_shapes=[
            pltpu.VMEM((rows,), f32),
            pltpu.VMEM((3 * points, points), bf16),
            pltpu.VMEM((fields, 2, depth, rows + 2 * PAD, half), f32),
            pltpu.VMEM((2,) + packs, f32),
            pltpu.VMEM((2,) + packs, f32),
            pltpu.VMEM((2,) + packs, f32),
            pltpu.SemaphoreType.REGULAR,
            pltpu.SemaphoreType.DMA(()),
            pltpu.SemaphoreType.DMA((2, parts)),
            pltpu.SemaphoreType.DMA((2, 2)),
            pltpu.SemaphoreType.DMA((2, 2)),
            pltpu.SemaphoreType.DMA((2, fields)),
            pltpu.SemaphoreType.DMA((2, fields)),
        ],
        compiler_params=pltpu.CompilerParams(
            collective_id=0, has_side_effects=True, vmem_limit_bytes=24 * 1024 * 1024
        ),
        name="local",
    )(
        pltpu.with_memory_space_constraint(velocity, pltpu.HBM),
        pltpu.with_memory_space_constraint(metric_y, pltpu.HBM),
    )
    return pl.pallas_call(
        finish_kernel,
        out_shape=(
            jax.ShapeDtypeStruct((fields, depth, rows, points), f32),
            jax.ShapeDtypeStruct((depth, rows, points), f32),
        ),
        in_specs=[vmem] * 5,
        out_specs=(anywhere, anywhere),
        scratch_shapes=[
            pltpu.VMEM((fields + 1, depth, rows, points), f32),
            pltpu.SemaphoreType.DMA((2,)),
        ],
        compiler_params=pltpu.CompilerParams(vmem_limit_bytes=24 * 1024 * 1024),
        name="finish",
    )(local, sheared, strips, spreads, metric_x)


def solution(mesh):
    in_specs = (P(None, None, "gy", "gx"), P("gx"), P("gy"))
    out_specs = (P(None, None, "gy", "gx"), P(None, "gy", "gx"))
    return jax.shard_map(
        per_device, mesh=mesh, in_specs=in_specs, out_specs=out_specs, check_vma=False
    )
```

```python
import numpy as np
import jax
import jax.numpy as jnp
from jax import lax
from jax.experimental import pallas as pl
from jax.experimental.pallas import tpu as pltpu
from jax.sharding import PartitionSpec as P

ratio = (np.sqrt(5.0) - 3.0) / 2.0
green = 1.0 / (1.0 + 2.0 * ratio / 3.0)
tail = green * 25.0 / 36.0
centre = green * (7.0 / 9.0 + ratio / 18.0)
MESH = pl.DeviceIdType.MESH
f32 = jnp.float32
bf16 = jnp.bfloat16
PAD = 8
LOAD_PARTS = 2
BATCH = 8
EDGE_PLANES = 4
MEET = 1
FINISH_PLANES = 4
BLOCK = 16
PER_TILE = 6
STRETCH = 1.8203296661376953


def powers_of_ratio(exponent, bits):
    value = jnp.ones(exponent.shape, f32)
    for bit in range(bits):
        factor = float(ratio ** (2**bit))
        factor = factor if abs(factor) > 1e-37 else 0.0
        value = value * jnp.where((exponent >> bit) & 1 == 1, factor, 1.0)
    return value


def halves(values):
    high = values.astype(bf16)
    return high, (values - high.astype(f32)).astype(bf16)


def band_matrix(points):
    source = lax.broadcasted_iota(jnp.int32, (points, points), 0)
    target = lax.broadcasted_iota(jnp.int32, (points, points), 1)
    distance = jnp.abs(target - source - 1)
    values = jnp.where(distance == 0, centre, tail * powers_of_ratio(distance, 7))
    return jnp.where((source < points - 2) & (distance < 128), values, 0.0)


def correction_matrix(points):
    half = points // 2
    source = lax.broadcasted_iota(jnp.int32, (points, points), 0)
    target = lax.broadcasted_iota(jnp.int32, (points, points), 1)
    distance = jnp.where(source < half, target, points - 1 - target)
    edge = jnp.where(distance == 0, 1.0, 0.0)
    decay = jnp.where(distance < 128, STRETCH * powers_of_ratio(distance, 7), 0.0)
    second = source % 2 == jnp.where(source < half, 1, 0)
    return jnp.where(second, edge, decay), source


def ring(axis):
    count = lax.axis_size(axis)
    me = lax.axis_index(axis)
    return lax.rem(me + 1, count), lax.rem(me + count - 1, count)


def local_kernel(
    velocity, metric_y, local, sheared, strips, spreads,
    my_line, band, held, sent, own, arrived,
    ready, my_sem, in_sem, y_send, y_recv, x_send, x_recv,
):
    fields, depth, rows, points = velocity.shape
    half = points // 2
    right, left = ring("gx")
    above, below = ring("gy")
    seam = lax.axis_index("gx") == 0
    last = lax.axis_index("gx") == lax.axis_size("gx") - 1
    planes = depth // LOAD_PARTS

    def load(side, part):
        field = part // LOAD_PARTS
        span = pl.ds((part % LOAD_PARTS) * planes, planes)
        return pltpu.make_async_copy(
            velocity.at[field, span, :, side * half : (side + 1) * half],
            held.at[field, side, span, PAD : PAD + rows],
            in_sem.at[side, part],
        )

    parts = fields * LOAD_PARTS
    for part in range(parts):
        load(1, part).start()
    barrier = pltpu.get_barrier_semaphore()
    for axis, place in (("gy", above), ("gy", below), ("gx", left)):
        pl.semaphore_signal(barrier, inc=1, device_id={axis: place}, device_id_type=MESH)

    @pl.when(jnp.logical_not(last))
    def greet_right():
        pl.semaphore_signal(barrier, inc=1, device_id={"gx": right}, device_id_type=MESH)

    my_load = pltpu.make_async_copy(metric_y, my_line, my_sem)

    high, low = halves(band_matrix(points))
    band[0:points] = high
    band[points : 2 * points] = high
    band[2 * points :] = low

    lane = lax.broadcasted_iota(jnp.int32, (8, half), 1)
    odd = lane % 2 == 1
    scale = tail * (1.0 + ratio)
    spread = scale * (1.0 - ratio)
    left_weight = jnp.where(lane == 0, -scale * ratio, spread * powers_of_ratio(lane, 7))
    right_weight = jnp.where(
        lane == half - 1, scale * ratio, -spread * powers_of_ratio(half - 1 - lane, 7)
    )

    def edges(side, after):
        weight = right_weight if side else left_weight

        def piece(part, carry):
            load(side, part).wait()
            if side:

                @pl.when(part == parts - 2)
                def start_others():
                    for other in range(parts):
                        load(0, other).start()
                    my_load.start()

            field = part // LOAD_PARTS

            def pair(step, carry):
                first = (part % LOAD_PARTS) * planes + step * EDGE_PLANES
                for z in [first + k for k in range(EDGE_PLANES)]:
                    groups = range(rows // 8)
                    blocks = [held[field, side, z, PAD + g * 8 : PAD + g * 8 + 8, :] for g in groups]
                    totals = [jnp.sum(block * weight, axis=1, keepdims=True) for block in blocks]
                    masks = [lane // 2 == within * 8 + z for within in range(PER_TILE)]
                    for group, block, total in zip(groups, blocks, totals):
                        tile, within = divmod(group // 2, PER_TILE)
                        edge = pltpu.roll(block, within * BLOCK + 2 * z + 2 * side, 1)
                        value = jnp.where(odd, edge, total) if side else jnp.where(odd, total, edge)
                        place = (side, field, tile, pl.ds((group % 2) * 8, 8))
                        pltpu.store(sent.at[place], value, mask=masks[within])
                        pltpu.store(own.at[place], edge, mask=masks[within])
                return carry

            return lax.fori_loop(0, planes // EDGE_PLANES, pair, carry)

        def whole(field, carry):
            lax.fori_loop(field * LOAD_PARTS, (field + 1) * LOAD_PARTS, piece, 0)
            after(field)
            return carry

        lax.fori_loop(0, fields, whole, 0)

    def x_copy(side, field):
        return pltpu.make_async_remote_copy(
            sent.at[side, field], arrived.at[1 - side, field],
            x_send.at[side, field], x_recv.at[1 - side, field],
            device_id={"gx": right if side else left}, device_id_type=MESH,
        )

    y_copies = [
        pltpu.make_async_remote_copy(
            velocity.at[0, :, first : first + PAD, side * half : (side + 1) * half],
            held.at[0, side, :, target : target + PAD],
            y_send.at[way, side], y_recv.at[way, side],
            device_id={"gy": place}, device_id_type=MESH,
        )
        for way, (first, target, place) in enumerate(
            ((rows - PAD, 0, above), (0, rows + PAD, below))
        )
        for side in range(2)
    ]

    def send_right(field):
        @pl.when(field == MEET)
        def meet():
            @pl.when(seam)
            def meet_three():
                pl.semaphore_wait(barrier, 3)

            @pl.when(jnp.logical_not(seam))
            def meet_four():
                pl.semaphore_wait(barrier, 4)

            @pl.when(last)
            def invite():
                pl.semaphore_signal(ready, inc=1, device_id={"gx": right}, device_id_type=MESH)

            for earlier in range(MEET):
                x_copy(1, earlier).start()

        @pl.when(field >= MEET)
        def send():
            x_copy(1, field).start()

    def send_left(field):
        @pl.when(field == 0)
        def first():
            for copy in y_copies:
                copy.start()

        @pl.when(jnp.logical_not(seam))
        def send():
            x_copy(0, field).start()

    edges(1, send_right)
    edges(0, send_left)

    decay, source = correction_matrix(points)
    for z in range(depth):
        spreads[z] = jnp.where(source // 2 % depth == z, decay, 0.0).astype(bf16)

    many = BATCH * rows
    def product(index, carry):
        field = index // (depth // BATCH)
        z = (index % (depth // BATCH)) * BATCH
        first = held[field, 0, pl.ds(z, BATCH), PAD : PAD + rows, :].reshape(many, half)
        second = held[field, 1, pl.ds(z, BATCH), PAD : PAD + rows, :].reshape(many, half)
        step = pltpu.roll(jnp.concatenate([first, second], axis=1), points - 2, 1)
        step = step - jnp.concatenate([first, second], axis=1)
        high, low = halves(step)
        result = jnp.dot(
            jnp.concatenate([high, low, high], axis=1), band[...], preferred_element_type=f32
        )
        local[field, pl.ds(z, BATCH)] = result.reshape(BATCH, rows, points)
        return carry

    my_load.wait()
    square = (
        lax.broadcasted_iota(jnp.int32, (rows, rows), 0)
        == lax.broadcasted_iota(jnp.int32, (rows, rows), 1)
    )
    my_row = my_line[...].reshape(1, rows)
    my_column = jnp.sum(jnp.where(square, my_row, 0.0), axis=1, keepdims=True) / 60.0

    def shear_rows(z, start, stop):
        for side in range(2):

            def shifted(k):
                return held[0, side, z, PAD + start + k : PAD + stop + k, :]

            sheared[z, start:stop, side * half : (side + 1) * half] = my_column[start:stop] * (
                45.0 * (shifted(1) - shifted(-1))
                - 9.0 * (shifted(2) - shifted(-2))
                + (shifted(3) - shifted(-3))
            )

    def shear_inner(z, carry):
        shear_rows(z, PAD, rows - PAD)
        return carry

    lax.fori_loop(0, depth, shear_inner, 0)

    lax.fori_loop(0, fields * depth // BATCH, product, 0)

    @pl.when(seam)
    def send_late():
        pl.semaphore_wait(ready, 1)
        for field in range(fields):
            x_copy(0, field).start()

    for copy in y_copies:
        copy.wait()

    for z in range(depth):
        shear_rows(z, 0, PAD)
        shear_rows(z, rows - PAD, rows)

    shape = arrived.shape[2:]
    small_odd = small_lanes(shape) % 2 == 1
    strip_lanes = small_lanes((BLOCK, half)) // BLOCK
    for side in (1, 0):
        turn, sign = (half - 1, 1.0) if side == 0 else (1, -1.0)
        for field in range(fields):
            x_copy(1 - side, field).wait_recv()
            far, near = arrived[side, field], own[side, field]
            straddle = sign * (near - far)
            jump = sign * (near - pltpu.roll(far, turn, 2))
            value = jnp.where(
                small_odd == (side == 0),
                (centre - tail) * straddle,
                (far + tail * pltpu.roll(straddle, turn, 2) + (tail * ratio) * jump)
                * (1.0 / STRETCH),
            )
            for block in range(rows // BLOCK):
                tile, within = divmod(block, PER_TILE)
                start = field * rows + block * BLOCK
                piece = jnp.where(strip_lanes == within, value[tile], 0.0)
                high, low = halves(piece)
                strips[start : start + BLOCK, side * half : (side + 1) * half] = high
                strips[start : start + BLOCK, points + side * half : points + (side + 1) * half] = low
    for side in range(2):
        for field in range(fields):
            x_copy(side, field).wait_send()


def small_lanes(shape):
    return lax.broadcasted_iota(jnp.int32, shape, len(shape) - 1)


def finish_kernel(
    local, sheared, strips, spreads, metric_x, derivs, vorticity, staged, out_sem
):
    fields, depth, rows, points = derivs.shape
    mx = metric_x[...].reshape(1, points)

    def copies(z):
        out = [
            pltpu.make_async_copy(staged.at[field, z], derivs.at[field, z], out_sem.at[0])
            for field in range(fields)
        ]
        out.append(pltpu.make_async_copy(staged.at[fields, z], vorticity.at[z], out_sem.at[1]))
        return out

    def planes(step, carry):
        for z in [step * FINISH_PLANES + k for k in range(FINISH_PLANES)]:
            sends = copies(z)
            for field in range(fields):
                span = slice(field * rows, (field + 1) * rows)
                change = jnp.dot(
                    strips[span, :points], spreads[z], preferred_element_type=f32
                ) + jnp.dot(strips[span, points:], spreads[z], preferred_element_type=f32)
                value = (local[field, z] + change) * mx
                staged[field, z] = value
                if field == 1:
                    staged[fields, z] = value - sheared[z]
            for copy in sends:
                copy.start()
        return carry

    lax.fori_loop(0, depth // FINISH_PLANES, planes, 0)

    pltpu.make_async_copy(staged.at[0:fields], derivs, out_sem.at[0]).wait()
    pltpu.make_async_copy(staged.at[fields], vorticity, out_sem.at[1]).wait()


def per_device(velocity, metric_x, metric_y):
    fields, depth, rows, points = velocity.shape
    half = points // 2
    packs = (fields, 2, BLOCK, half)
    parts = fields * LOAD_PARTS
    anywhere = pl.BlockSpec(memory_space=pl.ANY)
    hbm = pl.BlockSpec(memory_space=pltpu.HBM)
    vmem = pl.BlockSpec(memory_space=pltpu.VMEM)
    local, sheared, strips, spreads = pl.pallas_call(
        local_kernel,
        out_shape=(
            pltpu.VMEM((fields, depth, rows, points), f32),
            pltpu.VMEM((depth, rows, points), f32),
            pltpu.VMEM((fields * rows, 2 * points), bf16),
            pltpu.VMEM((depth, points, points), bf16),
        ),
        in_specs=[hbm, hbm],
        out_specs=(vmem,) * 4,
        scratch_shapes=[
            pltpu.VMEM((rows,), f32),
            pltpu.VMEM((3 * points, points), bf16),
            pltpu.VMEM((fields, 2, depth, rows + 2 * PAD, half), f32),
            pltpu.VMEM((2,) + packs, f32),
            pltpu.VMEM((2,) + packs, f32),
            pltpu.VMEM((2,) + packs, f32),
            pltpu.SemaphoreType.REGULAR,
            pltpu.SemaphoreType.DMA(()),
            pltpu.SemaphoreType.DMA((2, parts)),
            pltpu.SemaphoreType.DMA((2, 2)),
            pltpu.SemaphoreType.DMA((2, 2)),
            pltpu.SemaphoreType.DMA((2, fields)),
            pltpu.SemaphoreType.DMA((2, fields)),
        ],
        compiler_params=pltpu.CompilerParams(
            collective_id=0, has_side_effects=True, vmem_limit_bytes=24 * 1024 * 1024
        ),
        name="local",
    )(
        pltpu.with_memory_space_constraint(velocity, pltpu.HBM),
        pltpu.with_memory_space_constraint(metric_y, pltpu.HBM),
    )
    return pl.pallas_call(
        finish_kernel,
        out_shape=(
            jax.ShapeDtypeStruct((fields, depth, rows, points), f32),
            jax.ShapeDtypeStruct((depth, rows, points), f32),
        ),
        in_specs=[vmem] * 5,
        out_specs=(anywhere, anywhere),
        scratch_shapes=[
            pltpu.VMEM((fields + 1, depth, rows, points), f32),
            pltpu.SemaphoreType.DMA((2,)),
        ],
        compiler_params=pltpu.CompilerParams(vmem_limit_bytes=24 * 1024 * 1024),
        name="finish",
    )(local, sheared, strips, spreads, metric_x)


def solution(mesh):
    in_specs = (P(None, None, "gy", "gx"), P("gx"), P("gy"))
    out_specs = (P(None, None, "gy", "gx"), P(None, "gy", "gx"))
    return jax.shard_map(
        per_device, mesh=mesh, in_specs=in_specs, out_specs=out_specs, check_vma=False
    )
```

```python
import numpy as np
import jax
import jax.numpy as jnp
from jax import lax
from jax.experimental import pallas as pl
from jax.experimental.pallas import tpu as pltpu
from jax.sharding import PartitionSpec as P

ratio = (np.sqrt(5.0) - 3.0) / 2.0
green = 1.0 / (1.0 + 2.0 * ratio / 3.0)
tail = green * 25.0 / 36.0
centre = green * (7.0 / 9.0 + ratio / 18.0)
MESH = pl.DeviceIdType.MESH
f32 = jnp.float32
bf16 = jnp.bfloat16
PAD = 8
LOAD_PARTS = 2
BATCH = 8
EDGE_PLANES = 4
MEET = 1
FINISH_PLANES = 4
BLOCK = 16
PER_TILE = 6
STRETCH = 1.8203296661376953


def powers_of_ratio(exponent, bits):
    value = jnp.ones(exponent.shape, f32)
    for bit in range(bits):
        factor = float(ratio ** (2**bit))
        factor = factor if abs(factor) > 1e-37 else 0.0
        value = value * jnp.where((exponent >> bit) & 1 == 1, factor, 1.0)
    return value


def halves(values):
    high = values.astype(bf16)
    return high, (values - high.astype(f32)).astype(bf16)


def band_matrix(points):
    source = lax.broadcasted_iota(jnp.int32, (points, points), 0)
    target = lax.broadcasted_iota(jnp.int32, (points, points), 1)
    distance = jnp.abs(target - source - 1)
    values = jnp.where(distance == 0, centre, tail * powers_of_ratio(distance, 7))
    return jnp.where((source < points - 2) & (distance < 128), values, 0.0)


def correction_matrix(points):
    half = points // 2
    source = lax.broadcasted_iota(jnp.int32, (points, points), 0)
    target = lax.broadcasted_iota(jnp.int32, (points, points), 1)
    distance = jnp.where(source < half, target, points - 1 - target)
    edge = jnp.where(distance == 0, 1.0, 0.0)
    decay = jnp.where(distance < 128, STRETCH * powers_of_ratio(distance, 7), 0.0)
    second = source % 2 == jnp.where(source < half, 1, 0)
    return jnp.where(second, edge, decay), source


def ring(axis):
    count = lax.axis_size(axis)
    me = lax.axis_index(axis)
    return lax.rem(me + 1, count), lax.rem(me + count - 1, count)


def local_kernel(
    velocity, metric_y, local, sheared, strips, spreads,
    my_line, band, held, sent, own, arrived,
    ready, my_sem, in_sem, y_send, y_recv, x_send, x_recv,
):
    fields, depth, rows, points = velocity.shape
    half = points // 2
    right, left = ring("gx")
    above, below = ring("gy")
    seam = lax.axis_index("gx") == 0
    last = lax.axis_index("gx") == lax.axis_size("gx") - 1
    planes = depth // LOAD_PARTS

    def load(side, part):
        field = part // LOAD_PARTS
        span = pl.ds((part % LOAD_PARTS) * planes, planes)
        return pltpu.make_async_copy(
            velocity.at[field, span, :, side * half : (side + 1) * half],
            held.at[field, side, span, PAD : PAD + rows],
            in_sem.at[side, part],
        )

    parts = fields * LOAD_PARTS
    for part in range(parts):
        load(1, part).start()
    barrier = pltpu.get_barrier_semaphore()
    for axis, place in (("gy", above), ("gy", below), ("gx", left)):
        pl.semaphore_signal(barrier, inc=1, device_id={axis: place}, device_id_type=MESH)

    @pl.when(jnp.logical_not(last))
    def greet_right():
        pl.semaphore_signal(barrier, inc=1, device_id={"gx": right}, device_id_type=MESH)

    my_load = pltpu.make_async_copy(metric_y, my_line, my_sem)

    high, low = halves(band_matrix(points))
    band[0:points] = high
    band[points : 2 * points] = high
    band[2 * points :] = low

    lane = lax.broadcasted_iota(jnp.int32, (8, half), 1)
    odd = lane % 2 == 1
    scale = tail * (1.0 + ratio)
    spread = scale * (1.0 - ratio)
    left_weight = jnp.where(lane == 0, -scale * ratio, spread * powers_of_ratio(lane, 7))
    right_weight = jnp.where(
        lane == half - 1, scale * ratio, -spread * powers_of_ratio(half - 1 - lane, 7)
    )

    def edges(side, after):
        weight = right_weight if side else left_weight

        def piece(part, carry):
            load(side, part).wait()
            field = part // LOAD_PARTS

            def pair(step, carry):
                first = (part % LOAD_PARTS) * planes + step * EDGE_PLANES
                for z in [first + k for k in range(EDGE_PLANES)]:
                    groups = range(rows // 8)
                    blocks = [held[field, side, z, PAD + g * 8 : PAD + g * 8 + 8, :] for g in groups]
                    totals = [jnp.sum(block * weight, axis=1, keepdims=True) for block in blocks]
                    masks = [lane // 2 == within * 8 + z for within in range(PER_TILE)]
                    for group, block, total in zip(groups, blocks, totals):
                        tile, within = divmod(group // 2, PER_TILE)
                        edge = pltpu.roll(block, within * BLOCK + 2 * z + 2 * side, 1)
                        value = jnp.where(odd, edge, total) if side else jnp.where(odd, total, edge)
                        place = (side, field, tile, pl.ds((group % 2) * 8, 8))
                        pltpu.store(sent.at[place], value, mask=masks[within])
                        pltpu.store(own.at[place], edge, mask=masks[within])
                return carry

            return lax.fori_loop(0, planes // EDGE_PLANES, pair, carry)

        def whole(field, carry):
            lax.fori_loop(field * LOAD_PARTS, (field + 1) * LOAD_PARTS, piece, 0)
            after(field)
            return carry

        lax.fori_loop(0, fields, whole, 0)

    def x_copy(side, field):
        return pltpu.make_async_remote_copy(
            sent.at[side, field], arrived.at[1 - side, field],
            x_send.at[side, field], x_recv.at[1 - side, field],
            device_id={"gx": right if side else left}, device_id_type=MESH,
        )

    y_copies = [
        pltpu.make_async_remote_copy(
            velocity.at[0, :, first : first + PAD, side * half : (side + 1) * half],
            held.at[0, side, :, target : target + PAD],
            y_send.at[way, side], y_recv.at[way, side],
            device_id={"gy": place}, device_id_type=MESH,
        )
        for way, (first, target, place) in enumerate(
            ((rows - PAD, 0, above), (0, rows + PAD, below))
        )
        for side in range(2)
    ]

    def send_right(field):
        @pl.when(field == MEET)
        def meet():
            @pl.when(seam)
            def meet_three():
                pl.semaphore_wait(barrier, 3)

            @pl.when(jnp.logical_not(seam))
            def meet_four():
                pl.semaphore_wait(barrier, 4)

            @pl.when(last)
            def invite():
                pl.semaphore_signal(ready, inc=1, device_id={"gx": right}, device_id_type=MESH)

            for earlier in range(MEET):
                x_copy(1, earlier).start()

        @pl.when(field >= MEET)
        def send():
            x_copy(1, field).start()

    def send_left(field):
        @pl.when(field == 0)
        def first():
            for copy in y_copies:
                copy.start()

        @pl.when(jnp.logical_not(seam))
        def send():
            x_copy(0, field).start()

    for part in range(parts):
        load(0, part).start()
    my_load.start()
    edges(1, send_right)
    edges(0, send_left)

    decay, source = correction_matrix(points)
    for z in range(depth):
        spreads[z] = jnp.where(source // 2 % depth == z, decay, 0.0).astype(bf16)

    many = BATCH * rows
    def product(index, carry):
        field = index // (depth // BATCH)
        z = (index % (depth // BATCH)) * BATCH
        first = held[field, 0, pl.ds(z, BATCH), PAD : PAD + rows, :].reshape(many, half)
        second = held[field, 1, pl.ds(z, BATCH), PAD : PAD + rows, :].reshape(many, half)
        step = pltpu.roll(jnp.concatenate([first, second], axis=1), points - 2, 1)
        step = step - jnp.concatenate([first, second], axis=1)
        high, low = halves(step)
        result = jnp.dot(
            jnp.concatenate([high, low, high], axis=1), band[...], preferred_element_type=f32
        )
        local[field, pl.ds(z, BATCH)] = result.reshape(BATCH, rows, points)
        return carry

    my_load.wait()
    square = (
        lax.broadcasted_iota(jnp.int32, (rows, rows), 0)
        == lax.broadcasted_iota(jnp.int32, (rows, rows), 1)
    )
    my_row = my_line[...].reshape(1, rows)
    my_column = jnp.sum(jnp.where(square, my_row, 0.0), axis=1, keepdims=True) / 60.0

    def shear_rows(z, start, stop):
        for side in range(2):

            def shifted(k):
                return held[0, side, z, PAD + start + k : PAD + stop + k, :]

            sheared[z, start:stop, side * half : (side + 1) * half] = my_column[start:stop] * (
                45.0 * (shifted(1) - shifted(-1))
                - 9.0 * (shifted(2) - shifted(-2))
                + (shifted(3) - shifted(-3))
            )

    def shear_inner(z, carry):
        shear_rows(z, PAD, rows - PAD)
        return carry

    lax.fori_loop(0, depth, shear_inner, 0)

    lax.fori_loop(0, fields * depth // BATCH, product, 0)

    @pl.when(seam)
    def send_late():
        pl.semaphore_wait(ready, 1)
        for field in range(fields):
            x_copy(0, field).start()

    for copy in y_copies:
        copy.wait()

    for z in range(depth):
        shear_rows(z, 0, PAD)
        shear_rows(z, rows - PAD, rows)

    shape = arrived.shape[2:]
    small_odd = small_lanes(shape) % 2 == 1
    strip_lanes = small_lanes((BLOCK, half)) // BLOCK
    for side in (1, 0):
        turn, sign = (half - 1, 1.0) if side == 0 else (1, -1.0)
        for field in range(fields):
            x_copy(1 - side, field).wait_recv()
            far, near = arrived[side, field], own[side, field]
            straddle = sign * (near - far)
            jump = sign * (near - pltpu.roll(far, turn, 2))
            value = jnp.where(
                small_odd == (side == 0),
                (centre - tail) * straddle,
                (far + tail * pltpu.roll(straddle, turn, 2) + (tail * ratio) * jump)
                * (1.0 / STRETCH),
            )
            for block in range(rows // BLOCK):
                tile, within = divmod(block, PER_TILE)
                start = field * rows + block * BLOCK
                piece = jnp.where(strip_lanes == within, value[tile], 0.0)
                high, low = halves(piece)
                strips[start : start + BLOCK, side * half : (side + 1) * half] = high
                strips[start : start + BLOCK, points + side * half : points + (side + 1) * half] = low
    for side in range(2):
        for field in range(fields):
            x_copy(side, field).wait_send()


def small_lanes(shape):
    return lax.broadcasted_iota(jnp.int32, shape, len(shape) - 1)


def finish_kernel(
    local, sheared, strips, spreads, metric_x, derivs, vorticity, staged, out_sem
):
    fields, depth, rows, points = derivs.shape
    mx = metric_x[...].reshape(1, points)

    def copies(z):
        out = [
            pltpu.make_async_copy(staged.at[field, z], derivs.at[field, z], out_sem.at[0])
            for field in range(fields)
        ]
        out.append(pltpu.make_async_copy(staged.at[fields, z], vorticity.at[z], out_sem.at[1]))
        return out

    def planes(step, carry):
        for z in [step * FINISH_PLANES + k for k in range(FINISH_PLANES)]:
            sends = copies(z)
            for field in range(fields):
                span = slice(field * rows, (field + 1) * rows)
                change = jnp.dot(
                    strips[span, :points], spreads[z], preferred_element_type=f32
                ) + jnp.dot(strips[span, points:], spreads[z], preferred_element_type=f32)
                value = (local[field, z] + change) * mx
                staged[field, z] = value
                if field == 1:
                    staged[fields, z] = value - sheared[z]
            for copy in sends:
                copy.start()
        return carry

    lax.fori_loop(0, depth // FINISH_PLANES, planes, 0)

    pltpu.make_async_copy(staged.at[0:fields], derivs, out_sem.at[0]).wait()
    pltpu.make_async_copy(staged.at[fields], vorticity, out_sem.at[1]).wait()


def per_device(velocity, metric_x, metric_y):
    fields, depth, rows, points = velocity.shape
    half = points // 2
    packs = (fields, 2, BLOCK, half)
    parts = fields * LOAD_PARTS
    anywhere = pl.BlockSpec(memory_space=pl.ANY)
    hbm = pl.BlockSpec(memory_space=pltpu.HBM)
    vmem = pl.BlockSpec(memory_space=pltpu.VMEM)
    local, sheared, strips, spreads = pl.pallas_call(
        local_kernel,
        out_shape=(
            pltpu.VMEM((fields, depth, rows, points), f32),
            pltpu.VMEM((depth, rows, points), f32),
            pltpu.VMEM((fields * rows, 2 * points), bf16),
            pltpu.VMEM((depth, points, points), bf16),
        ),
        in_specs=[hbm, hbm],
        out_specs=(vmem,) * 4,
        scratch_shapes=[
            pltpu.VMEM((rows,), f32),
            pltpu.VMEM((3 * points, points), bf16),
            pltpu.VMEM((fields, 2, depth, rows + 2 * PAD, half), f32),
            pltpu.VMEM((2,) + packs, f32),
            pltpu.VMEM((2,) + packs, f32),
            pltpu.VMEM((2,) + packs, f32),
            pltpu.SemaphoreType.REGULAR,
            pltpu.SemaphoreType.DMA(()),
            pltpu.SemaphoreType.DMA((2, parts)),
            pltpu.SemaphoreType.DMA((2, 2)),
            pltpu.SemaphoreType.DMA((2, 2)),
            pltpu.SemaphoreType.DMA((2, fields)),
            pltpu.SemaphoreType.DMA((2, fields)),
        ],
        compiler_params=pltpu.CompilerParams(
            collective_id=0, has_side_effects=True, vmem_limit_bytes=24 * 1024 * 1024
        ),
        name="local",
    )(
        pltpu.with_memory_space_constraint(velocity, pltpu.HBM),
        pltpu.with_memory_space_constraint(metric_y, pltpu.HBM),
    )
    return pl.pallas_call(
        finish_kernel,
        out_shape=(
            jax.ShapeDtypeStruct((fields, depth, rows, points), f32),
            jax.ShapeDtypeStruct((depth, rows, points), f32),
        ),
        in_specs=[vmem] * 5,
        out_specs=(anywhere, anywhere),
        scratch_shapes=[
            pltpu.VMEM((fields + 1, depth, rows, points), f32),
            pltpu.SemaphoreType.DMA((2,)),
        ],
        compiler_params=pltpu.CompilerParams(vmem_limit_bytes=24 * 1024 * 1024),
        name="finish",
    )(local, sheared, strips, spreads, metric_x)


def solution(mesh):
    in_specs = (P(None, None, "gy", "gx"), P("gx"), P("gy"))
    out_specs = (P(None, None, "gy", "gx"), P(None, "gy", "gx"))
    return jax.shard_map(
        per_device, mesh=mesh, in_specs=in_specs, out_specs=out_specs, check_vma=False
    )
```
